32 devices in a mesh: gx: 4 (over x, core), gz: 8 (over z, y).
Axes of the slice: x: 2, y: 2, z: 4, core: 2. Of those that a mesh axis runs over, the one named last changes fastest.
Arguments:
- velocity: float32 [3, 2048, 8, 2048], P(None, 'gx', None, 'gz'), may hold values from -32 to 32
Outputs:
- grad_x: float32 [3, 2048, 8, 2048], P(None, 'gx', None, 'gz')
- grad_z: float32 [3, 2048, 8, 2048], P(None, 'gx', None, 'gz')
- convect: float32 [3, 2048, 8, 2048], P(None, 'gx', None, 'gz')
- rebuilt: float32 [2, 2048, 8, 2048], P(None, 'gx', None, 'gz')
The draws below stay inside these ranges and needn't reach their ends.
All inputs are finite; a program needn't handle non-finite values.
Results may differ from the reference program's by a relative error of at most 0.0003.
Values sent between devices are 32-bit elements; how exact they have to be, the bound alone decides.
A program may use at most 256 MiB of HBM per device.

```python
import math
import jax
import jax.numpy as jnp
from jax import lax

NX = 2048
NZ = 2048
Y = 8


def draw_velocity(key, part):
    noise_key, xrough_key, zrough_key = jax.random.split(jax.random.fold_in(key, 17), 3)
    x_frac = jnp.arange(NX, dtype=jnp.float32) / NX
    z_frac = jnp.arange(NZ, dtype=jnp.float32) / NZ
    rough_x = jax.random.uniform(xrough_key, (3, NX), jnp.float32, -0.35, 0.35)
    rough_z = jax.random.uniform(zrough_key, (3, NZ), jnp.float32, -0.35, 0.35)
    growth = math.log(3.0)
    noise = jax.random.truncated_normal(noise_key, -4.0, 4.0, (3, NX, Y, NZ), jnp.float32)
    norm_factor = growth / (math.exp(growth) - 1.0)
    scale_x = jnp.exp(growth * x_frac[None, :] + rough_x) * norm_factor
    scale_z = jnp.exp(growth * z_frac[None, :] + rough_z) * norm_factor
    value = noise * scale_x[:, :, None, None] * scale_z[:, None, None, :]
    return value


def setup_inputs(seed: int = 0) -> dict:
    key_of = jax.random.split(jax.random.key(seed), 2)
    velocity = draw_velocity(jax.random.fold_in(key_of[1], 71), 0)
    return dict(velocity=velocity)


ALPHA = 1.0 / 3.0
COEF_A = 14.0 / 9.0
COEF_B = 1.0 / 9.0

def derivative(field, axis_at):
    length = field.shape[axis_at]
    spectrum = jnp.fft.rfft(field, axis=axis_at)
    wave = 2.0 * math.pi * jnp.arange(length // 2 + 1).astype(field.dtype) / length
    factor = (COEF_A * jnp.sin(wave) + 0.5 * COEF_B * jnp.sin(2.0 * wave)) / (1.0 + 2.0 * ALPHA * jnp.cos(wave))
    shape_list = [1] * field.ndim
    shape_list[axis_at] = length // 2 + 1
    result = jnp.fft.irfft(spectrum * (1j * factor.reshape(shape_list)), n=length, axis=axis_at)
    return result.astype(field.dtype)

def primitive(values, axis_at):
    length = values.shape[axis_at]
    shape_list = [1] * values.ndim
    shape_list[axis_at] = length
    position = jnp.arange(length).astype(values.dtype).reshape(shape_list)
    mean_value = lax.optimization_barrier(jnp.mean(values, axis=axis_at, keepdims=True))
    centred_sum = lax.optimization_barrier(jnp.sum(values * (position - 0.5 * (length - 1)), axis=axis_at, keepdims=True))
    running = jnp.cumsum(values, axis=axis_at)
    zero_slice = jnp.zeros_like(lax.slice_in_dim(values, 0, 1, axis=axis_at))
    before = jnp.concatenate([zero_slice, lax.slice_in_dim(running, 0, length - 1, axis=axis_at)], axis_at)
    result = before - position * mean_value + 0.5 * (values - mean_value) + centred_sum / length
    return -result / math.sqrt(length)

def reference(velocity):
    along_x = []
    along_z = []
    fluxes = []
    for comp in range(3):
        field = velocity[comp]
        along_x.append(derivative(field, 0))
        along_z.append(derivative(field, 2))
        flux_x = velocity[0] * field
        flux_z = velocity[2] * field
        fluxes.append(derivative(flux_x, 0) + derivative(flux_z, 2))
    rebuilt = jnp.stack([primitive(along_z[2], 0), primitive(along_x[0], 2)])
    return (jnp.stack(along_x), jnp.stack(along_z), jnp.stack(fluxes), rebuilt)
```

```python
import functools
import math

import jax
import jax.numpy as jnp
import ml_dtypes
import numpy as np
from jax import lax
from jax.experimental import pallas as pl
from jax.experimental.pallas import tpu as pltpu
from jax.sharding import PartitionSpec as P

ROOT = (math.sqrt(5.0) - 3.0) / 2.0
C = 25.0 / 12.0
KAPPA = -1.0 / 12.0
TX = 64
STEP = 4
F32 = jnp.float32
BF16 = jnp.bfloat16
LIMIT = 52 * 1024 * 1024
MESH = pl.DeviceIdType.MESH


def halves(array):
    high = array.astype(ml_dtypes.bfloat16)
    low = (array - high.astype(np.float64)).astype(ml_dtypes.bfloat16)
    return high, low


def split(value):
    high = value.astype(BF16)
    low = (value - high.astype(F32)).astype(BF16)
    return high, low


def mm(left, right):
    return jnp.dot(left, right, preferred_element_type=F32)


def kernel_values(offset):
    size = np.abs(offset)
    power = np.power(np.abs(ROOT), size) * np.where(size % 2 == 0, 1.0, -1.0)
    value = np.sign(offset) * C * power
    return value + np.where(size == 1, np.sign(offset) * KAPPA, 0.0)


def signed_power(exponent):
    return np.power(np.abs(ROOT), exponent) * np.where(exponent % 2 == 0, 1.0, -1.0)


def derivative_matrices(cz):
    at = np.arange(cz)
    return halves(kernel_values(at[None, :] - at[:, None]))


def edge_weights(cz):
    at = np.arange(cz)
    out = np.zeros((6, cz, 128))
    low_out = np.zeros((6, cz, 128))
    for f in range(6):
        base = np.zeros((cz, 32))
        base[:, f] = signed_power(cz - at)
        base[cz - 1, 6 + f] = 1.0
        base[:, 16 + f] = signed_power(at + 1)
        base[0, 22 + f] = 1.0
        high, low = halves(base)
        out[f, :, 0:32] = high.astype(np.float64)
        out[f, :, 32:64] = low.astype(np.float64)
        low_out[f, :, 0:32] = high.astype(np.float64)
    return out.astype(ml_dtypes.bfloat16), low_out.astype(ml_dtypes.bfloat16)


def correction_matrices(cz):
    at = np.arange(cz)
    out = np.zeros((6, 128, cz))
    for f in range(6):
        base = np.zeros((32, cz))
        base[f] = C * signed_power(at)
        base[6 + f, 0] = KAPPA
        base[16 + f] = -C * signed_power(cz - 1 - at)
        base[22 + f, cz - 1] = -KAPPA
        high, low = halves(base)
        out[f, 0:32] = high.astype(np.float64)
        out[f, 32:64] = high.astype(np.float64)
        out[f, 64:96] = low.astype(np.float64)
    return out.astype(ml_dtypes.bfloat16)


def fields(planes, pivot):
    return list(planes) + [planes[pivot] * p for p in planes]


def edges_kernel(steps, v_ref, wa_ref, wb_ref, ck_ref, xup_ref, xdn_ref, zup_ref, zdn_ref, back, fore):
    s = pl.program_id(0)
    cz = v_ref.shape[3]
    rows = TX * 8

    @pl.when(s == 0)
    def _():
        back[...] = jnp.zeros_like(back)
        fore[...] = jnp.zeros_like(fore)
        xup_ref[6:9] = v_ref[:, TX - 1]

    ck_ref[0] = back[...]

    def sweep(k, state):
        states = list(state)
        for j in range(STEP):
            i = TX - 1 - (k * STEP + j)
            now = fields([v_ref[c, i] for c in range(3)], 0)
            states = [ROOT * (f + b) for f, b in zip(now, states)]
        return tuple(states)

    final = lax.fori_loop(0, TX // STEP, sweep, tuple(back[c] for c in range(6)))
    for c in range(6):
        back[c] = final[c]
    back[6:9] = v_ref[:, 0]

    @pl.when(s * TX < 128)
    def _():
        def ahead(k, state):
            states = list(state)
            for j in range(STEP):
                i = k * STEP + j
                now = fields([v_ref[c, i] for c in range(3)], 0)
                states = [ROOT * (f + b) for f, b in zip(now, states)]
            return tuple(states)

        zero = jnp.zeros((8, cz), F32)
        ended = lax.fori_loop(0, TX // STEP, ahead, (zero,) * 6)
        scale = jnp.where(s == 0, F32(1.0), F32(ROOT**TX))
        for c in range(6):
            fore[c] = fore[c] + scale * ended[c]

    planes = [v_ref[c].reshape(rows, cz) for c in range(3)]
    total = jnp.zeros((rows, 128), F32)
    for f in range(6):
        value = planes[f] if f < 3 else planes[2] * planes[f - 3]
        high, low = split(value)
        total = total + mm(high, wa_ref[f]) + mm(low, wb_ref[f])
    turned = total.T
    message = turned[0:32] + turned[32:64]
    zup_ref[...] = message[0:16]
    zdn_ref[...] = message[16:32]

    @pl.when(s == steps - 1)
    def _():
        xup_ref[0:6] = fore[...]
        xdn_ref[...] = back[...]


def find_edges(velocity):
    _, cx, ny, cz = velocity.shape
    steps = cx // TX
    rows = TX * 8
    wa, wb = edge_weights(cz)
    whole = lambda shape: pl.BlockSpec(shape, lambda s: (0,) * len(shape))
    turned = lambda s: (0, steps - 1 - s)
    return pl.pallas_call(
        functools.partial(edges_kernel, steps),
        grid=(steps,),
        in_specs=[
            pl.BlockSpec((3, TX, 8, cz), lambda s: (0, steps - 1 - s, 0, 0)),
            whole((6, cz, 128)),
            whole((6, cz, 128)),
        ],
        out_specs=[
            pl.BlockSpec((1, 9, 8, cz), lambda s: (steps - 1 - s, 0, 0, 0)),
            whole((9, 8, cz)),
            whole((9, 8, cz)),
            pl.BlockSpec((16, rows), turned),
            pl.BlockSpec((16, rows), turned),
        ],
        out_shape=[
            jax.ShapeDtypeStruct((steps, 9, 8, cz), F32),
            jax.ShapeDtypeStruct((9, 8, cz), F32),
            jax.ShapeDtypeStruct((9, 8, cz), F32),
            jax.ShapeDtypeStruct((16, cx * 8), F32),
            jax.ShapeDtypeStruct((16, cx * 8), F32),
        ],
        scratch_shapes=[pltpu.VMEM((9, 8, cz), F32), pltpu.VMEM((6, 8, cz), F32)],
        compiler_params=pltpu.CompilerParams(
            dimension_semantics=("arbitrary",), vmem_limit_bytes=LIMIT
        ),
        name="find_edges",
    )(velocity, jnp.asarray(wa), jnp.asarray(wb))


def neighbours_kernel(gx, gz, xup, xdn, zup, zdn, xl, xr, zl, zr, send_sem, recv_sem):
    mx, mz = lax.axis_index("gx"), lax.axis_index("gz")
    xnext = (lax.rem(mx + 1, gx), mz)
    xlast = (lax.rem(mx + gx - 1, gx), mz)
    znext = (mx, lax.rem(mz + 1, gz))
    zlast = (mx, lax.rem(mz + gz - 1, gz))
    barrier = pltpu.get_barrier_semaphore()
    for peer in (xnext, xlast, znext, zlast):
        pl.semaphore_signal(barrier, inc=1, device_id=peer, device_id_type=MESH)
    pl.semaphore_wait(barrier, 4)
    moves = ((zup, zl, znext), (zdn, zr, zlast), (xup, xl, xnext), (xdn, xr, xlast))
    copies = []
    for k, (src, dst, peer) in enumerate(moves):
        copy = pltpu.make_async_remote_copy(
            src_ref=src,
            dst_ref=dst,
            send_sem=send_sem.at[k],
            recv_sem=recv_sem.at[k],
            device_id=peer,
            device_id_type=MESH,
        )
        copy.start()
        copies.append(copy)
    for copy in copies:
        copy.wait()


def swap_edges(xup, xdn, zup, zdn):
    gx, gz = lax.axis_size("gx"), lax.axis_size("gz")
    shapes = [jax.ShapeDtypeStruct(a.shape, F32) for a in (xup, xdn, zup, zdn)]
    return pl.pallas_call(
        functools.partial(neighbours_kernel, gx, gz),
        in_specs=[pl.BlockSpec(memory_space=pl.ANY)] * 4,
        out_specs=[pl.BlockSpec(memory_space=pl.ANY)] * 4,
        out_shape=shapes,
        scratch_shapes=[pltpu.SemaphoreType.DMA((4,)), pltpu.SemaphoreType.DMA((4,))],
        compiler_params=pltpu.CompilerParams(collective_id=0, has_side_effects=True),
        name="swap_edges",
    )(xup, xdn, zup, zdn)


def main_kernel(
    steps, rp_ref, v_ref, ck_ref, xl_ref, xr_ref, zl_ref, zr_ref, kh_ref, kl_ref, cm_ref, sm_ref,
    gx_ref, gz_ref, cv_ref, xs_ref, zs_ref, held, fore,
):
    t = pl.program_id(0)
    cz = v_ref.shape[3]
    rows = TX * 8

    @pl.when(t == 0)
    def _():
        fore[...] = xl_ref[...]
        xs_ref[...] = jnp.zeros_like(xs_ref)

    parts = jnp.concatenate([zl_ref[...], zr_ref[...]], 0)
    high = parts.astype(BF16).astype(F32)
    low = parts - high
    message = jnp.concatenate([high, low, high, jnp.zeros_like(high)], 0).T.astype(BF16)
    planes = [v_ref[c].reshape(rows, cz) for c in range(3)]
    for f in range(6):
        value = planes[f] if f < 3 else planes[2] * planes[f - 3]
        hi, lo = split(value)
        slope = mm(hi, kh_ref[...]) + mm(hi, kl_ref[...]) + mm(lo, kh_ref[...])
        slope = slope + mm(message, cm_ref[f])
        target = gz_ref if f < 3 else cv_ref
        target[f % 3] = slope.reshape(TX, 8, cz)

    tail = rp_ref[t]
    last = t == steps - 1
    after = [jnp.where(last, xr_ref[6 + c], ck_ref[0, 6 + c]) for c in range(3)]
    start = [ck_ref[0, c] + tail * xr_ref[c] for c in range(6)]

    def backward(k, state):
        states, nexts = list(state[:6]), list(state[6:])
        for j in range(STEP):
            i = TX - 1 - (k * STEP + j)
            for f in range(6):
                held[f, i] = -C * states[f] - KAPPA * nexts[f]
            nexts = fields([v_ref[c, i] for c in range(3)], 0)
            states = [ROOT * (f + b) for f, b in zip(nexts, states)]
        return tuple(states) + tuple(nexts)

    lax.fori_loop(0, TX // STEP, backward, tuple(start) + tuple(fields(after, 0)))

    def forward(k, state):
        states, befores = list(state[:6]), list(state[6:12])
        sums, moments = state[12], state[13]
        for j in range(STEP):
            i = k * STEP + j
            for f in range(6):
                slope = C * states[f] + (KAPPA * befores[f] + held[f, i])
                if f < 3:
                    gx_ref[f, i] = slope
                else:
                    cv_ref[f - 3, i] = cv_ref[f - 3, i] + slope
            befores = fields([v_ref[c, i] for c in range(3)], 0)
            states = [ROOT * (f + b) for f, b in zip(befores, states)]
            w_slope = gz_ref[2, i]
            sums = sums + w_slope
            moments = moments + (t * TX + i).astype(F32) * w_slope
        return tuple(states) + tuple(befores) + (sums, moments)

    begin = tuple(fore[c] for c in range(6)) + tuple(fields([fore[6 + c] for c in range(3)], 0))
    ended = lax.fori_loop(0, TX // STEP, forward, begin + (xs_ref[0], xs_ref[1]))
    for c in range(6):
        fore[c] = ended[c]
    for c in range(3):
        fore[6 + c] = ended[6 + c]
    xs_ref[0] = ended[12]
    xs_ref[1] = ended[13]

    hi, lo = split(gx_ref[0].reshape(rows, cz))
    sums = (mm(hi, sm_ref[...]) + mm(lo, sm_ref[...])).T
    chunks = [sums[q : q + 1, 128 * k : 128 * k + 128] for q in range(2) for k in range(rows // 128)]
    zs_ref[0] = jnp.concatenate(chunks, 0)


def differentiate(velocity, ck, xl, xr, zl, zr):
    _, cx, ny, cz = velocity.shape
    steps = cx // TX
    rows = TX * 8
    kh, kl = derivative_matrices(cz)
    cm = correction_matrices(cz)
    sm = np.zeros((cz, 128), ml_dtypes.bfloat16)
    sm[:, 0] = 1.0
    sm[:, 1] = np.arange(cz)
    powers = signed_power(TX * (steps - 1 - np.arange(steps))).astype(np.float32)
    whole = lambda shape: pl.BlockSpec(shape, lambda t: (0,) * len(shape))
    tile = pl.BlockSpec((3, TX, 8, cz), lambda t: (0, t, 0, 0))
    line = pl.BlockSpec((16, rows), lambda t: (0, t))
    full = jax.ShapeDtypeStruct(velocity.shape, F32)
    return pl.pallas_call(
        functools.partial(main_kernel, steps),
        grid=(steps,),
        in_specs=[
            pl.BlockSpec(memory_space=pltpu.SMEM),
            tile,
            pl.BlockSpec((1, 9, 8, cz), lambda t: (t, 0, 0, 0)),
            whole((9, 8, cz)),
            whole((9, 8, cz)),
            line,
            line,
            whole((cz, cz)),
            whole((cz, cz)),
            whole((6, 128, cz)),
            whole((cz, 128)),
        ],
        out_specs=[
            tile,
            tile,
            tile,
            whole((2, 8, cz)),
            pl.BlockSpec((1, rows // 64, 128), lambda t: (t, 0, 0)),
        ],
        out_shape=[
            full,
            full,
            full,
            jax.ShapeDtypeStruct((2, 8, cz), F32),
            jax.ShapeDtypeStruct((steps, rows // 64, 128), F32),
        ],
        scratch_shapes=[pltpu.VMEM((6, TX, 8, cz), F32), pltpu.VMEM((9, 8, cz), F32)],
        compiler_params=pltpu.CompilerParams(
            dimension_semantics=("arbitrary",), vmem_limit_bytes=LIMIT
        ),
        name="differentiate",
    )(
        jnp.asarray(powers), velocity, ck, xl, xr, zl, zr,
        jnp.asarray(kh), jnp.asarray(kl), jnp.asarray(cm), jnp.asarray(sm),
    )


def gather_kernel(gx, gz, xs, zs, xg, zg, own_sem, send_x, recv_x, send_z, recv_z):
    mx, mz = lax.axis_index("gx"), lax.axis_index("gz")
    xpeers = [(lax.rem(mx + k, gx), mz) for k in range(1, gx)]
    zpeers = [(mx, lax.rem(mz + k, gz)) for k in range(1, gz)]
    barrier = pltpu.get_barrier_semaphore()
    for peer in xpeers + zpeers:
        pl.semaphore_signal(barrier, inc=1, device_id=peer, device_id_type=MESH)
    own = [
        pltpu.make_async_copy(xs, xg.at[mx], own_sem.at[0]),
        pltpu.make_async_copy(zs, zg.at[mz], own_sem.at[1]),
    ]
    for copy in own:
        copy.start()
    pl.semaphore_wait(barrier, gx + gz - 2)
    copies = []
    for src, dst, mine, peers, sends, recvs in (
        (zs, zg, mz, zpeers, send_z, recv_z),
        (xs, xg, mx, xpeers, send_x, recv_x),
    ):
        for k, peer in enumerate(peers):
            copy = pltpu.make_async_remote_copy(
                src_ref=src,
                dst_ref=dst.at[mine],
                send_sem=sends.at[k],
                recv_sem=recvs.at[k],
                device_id=peer,
                device_id_type=MESH,
            )
            copy.start()
            copies.append(copy)
    for copy in own + copies:
        copy.wait()


def gather_sums(xs, zs):
    gx, gz = lax.axis_size("gx"), lax.axis_size("gz")
    dma = pltpu.SemaphoreType.DMA
    return pl.pallas_call(
        functools.partial(gather_kernel, gx, gz),
        in_specs=[pl.BlockSpec(memory_space=pl.ANY)] * 2,
        out_specs=[pl.BlockSpec(memory_space=pl.ANY)] * 2,
        out_shape=[
            jax.ShapeDtypeStruct((gx,) + xs.shape, F32),
            jax.ShapeDtypeStruct((gz,) + zs.shape, F32),
        ],
        scratch_shapes=[
            dma((2,)), dma((gx - 1,)), dma((gx - 1,)), dma((gz - 1,)), dma((gz - 1,))
        ],
        compiler_params=pltpu.CompilerParams(collective_id=1, has_side_effects=True),
        name="gather_sums",
    )(xs, zs)


def rebuild_kernel(
    nx, nz, wx_ref, wz_ref, xg_ref, zg_ref, tm_ref, pm_ref, gzw_ref, gxu_ref, out_ref, run, mean
):
    t = pl.program_id(0)
    cz = gzw_ref.shape[3]
    rows = TX * 8
    scale_x, scale_z = -1.0 / math.sqrt(nx), -1.0 / math.sqrt(nz)

    @pl.when(t == 0)
    def _():
        base = jnp.zeros((8, cz), F32)
        average = jnp.zeros((8, cz), F32)
        for d in range(xg_ref.shape[0]):
            base = base + wx_ref[d] * xg_ref[d, 0] + xg_ref[d, 1] * (1.0 / nx)
            average = average + xg_ref[d, 0] * (1.0 / nx)
        run[...] = base
        mean[...] = average

    average = mean[...]

    def forward(k, total):
        for j in range(STEP):
            i = k * STEP + j
            value = gzw_ref[0, i]
            out_ref[0, i] = scale_x * (total + 0.5 * value)
            total = total + (value - average)
        return total

    run[...] = lax.fori_loop(0, TX // STEP, forward, run[...])

    chunks = rows // 128
    base = jnp.zeros((chunks, 128), F32)
    slope = jnp.zeros((chunks, 128), F32)
    for d in range(zg_ref.shape[0]):
        block = zg_ref[d, 0]
        base = base + wz_ref[d] * block[0:chunks] + block[chunks:] * (1.0 / nz)
        slope = slope + block[0:chunks] * (1.0 / nz)
    base = jnp.concatenate([base[k : k + 1] for k in range(chunks)], 1)
    slope = jnp.concatenate([slope[k : k + 1] for k in range(chunks)], 1)
    base_high = base.astype(BF16).astype(F32)
    slope_high = slope.astype(BF16).astype(F32)
    stacked = jnp.concatenate(
        [base_high, base - base_high, slope_high, slope - slope_high, jnp.zeros((124, rows), F32)], 0
    )
    message = stacked.T.astype(BF16)
    hi, lo = split(gxu_ref[0].reshape(rows, cz))
    result = mm(hi, tm_ref[...]) + mm(lo, tm_ref[...]) + mm(message, pm_ref[...])
    out_ref[1] = (scale_z * result).reshape(TX, 8, cz)


def start_weights(axis, cells):
    peers, mine = lax.axis_size(axis), lax.axis_index(axis)
    total = peers * cells
    at = jnp.arange(peers)
    starts = (at * cells - mine * cells).astype(F32)
    return (at < mine).astype(F32) + (starts - 0.5 * (total - 1) - 0.5) * (1.0 / total)


def rebuild(grad_x, grad_z, xg, zg):
    _, cx, ny, cz = grad_x.shape
    gx, gz = xg.shape[0], zg.shape[0]
    steps = cx // TX
    rows = TX * 8
    at = np.arange(cz)
    tm = (at[:, None] < at[None, :]) + 0.5 * (at[:, None] == at[None, :])
    pm = np.zeros((128, cz))
    pm[0:2] = 1.0
    pm[2:4] = -at
    whole = lambda shape: pl.BlockSpec(shape, lambda t: (0,) * len(shape))
    return pl.pallas_call(
        functools.partial(rebuild_kernel, cx * gx, cz * gz),
        grid=(steps,),
        in_specs=[
            pl.BlockSpec(memory_space=pltpu.SMEM),
            pl.BlockSpec(memory_space=pltpu.SMEM),
            whole((gx, 2, 8, cz)),
            pl.BlockSpec((gz, 1, rows // 64, 128), lambda t: (0, t, 0, 0)),
            whole((cz, cz)),
            whole((128, cz)),
            pl.BlockSpec((1, TX, 8, cz), lambda t: (2, t, 0, 0)),
            pl.BlockSpec((1, TX, 8, cz), lambda t: (0, t, 0, 0)),
        ],
        out_specs=pl.BlockSpec((2, TX, 8, cz), lambda t: (0, t, 0, 0)),
        out_shape=jax.ShapeDtypeStruct((2, cx, 8, cz), F32),
        scratch_shapes=[pltpu.VMEM((8, cz), F32), pltpu.VMEM((8, cz), F32)],
        compiler_params=pltpu.CompilerParams(
            dimension_semantics=("arbitrary",), vmem_limit_bytes=LIMIT
        ),
        name="rebuild",
    )(
        start_weights("gx", cx), start_weights("gz", cz), xg, zg,
        jnp.asarray(tm.astype(ml_dtypes.bfloat16)), jnp.asarray(pm.astype(ml_dtypes.bfloat16)),
        grad_z, grad_x,
    )


def body(velocity):
    ck, xup, xdn, zup, zdn = find_edges(velocity)
    xl, xr, zl, zr = swap_edges(xup, xdn, zup, zdn)
    grad_x, grad_z, convect, xs, zs = differentiate(velocity, ck, xl, xr, zl, zr)
    xg, zg = gather_sums(xs, zs)
    rebuilt = rebuild(grad_x, grad_z, xg, zg)
    return grad_x, grad_z, convect, rebuilt


def solution(mesh):
    placed = P(None, "gx", None, "gz")
    return jax.shard_map(
        body, mesh=mesh, in_specs=(placed,), out_specs=(placed,) * 4, check_vma=False
    )
```

```python
import functools
import math

import jax
import jax.numpy as jnp
import ml_dtypes
import numpy as np
from jax import lax
from jax.experimental import pallas as pl
from jax.experimental.pallas import tpu as pltpu
from jax.sharding import PartitionSpec as P

ROOT = (math.sqrt(5.0) - 3.0) / 2.0
C = 25.0 / 12.0
KAPPA = -1.0 / 12.0
TX = 64
CHUNK = 16
STEP = 8
F32 = jnp.float32
BF16 = jnp.bfloat16
LIMIT = 52 * 1024 * 1024
MESH = pl.DeviceIdType.MESH


def halves(array):
    high = array.astype(ml_dtypes.bfloat16)
    low = (array - high.astype(np.float64)).astype(ml_dtypes.bfloat16)
    return high, low


def split(value):
    high = value.astype(BF16)
    low = (value - high.astype(F32)).astype(BF16)
    return high, low


def mm(left, right):
    return jnp.dot(left, right, preferred_element_type=F32)


def kernel_values(offset):
    size = np.abs(offset)
    power = np.power(np.abs(ROOT), size) * np.where(size % 2 == 0, 1.0, -1.0)
    value = np.sign(offset) * C * power
    return value + np.where(size == 1, np.sign(offset) * KAPPA, 0.0)


def signed_power(exponent):
    return np.power(np.abs(ROOT), exponent) * np.where(exponent % 2 == 0, 1.0, -1.0)


def derivative_matrices(cz):
    at = np.arange(cz)
    return halves(kernel_values(at[None, :] - at[:, None]))


def edge_weights(cz):
    at = np.arange(cz)
    base = np.zeros((cz, 32))
    base[:, 0] = signed_power(cz - at)
    base[cz - 1, 6] = 1.0
    base[:, 16] = signed_power(at + 1)
    base[0, 22] = 1.0
    high, low = halves(base)
    out = np.zeros((cz, 128), np.float32)
    out[:, 0:32] = high.astype(np.float32)
    out[:, 32:64] = low.astype(np.float32)
    return out


def correction_matrices(cz):
    at = np.arange(cz)
    out = np.zeros((6, 128, cz))
    for f in range(6):
        base = np.zeros((32, cz))
        base[f] = C * signed_power(at)
        base[6 + f, 0] = KAPPA
        base[16 + f] = -C * signed_power(cz - 1 - at)
        base[22 + f, cz - 1] = -KAPPA
        high, low = halves(base)
        out[f, 0:32] = high.astype(np.float64)
        out[f, 32:64] = high.astype(np.float64)
        out[f, 64:96] = low.astype(np.float64)
    return out.astype(ml_dtypes.bfloat16)


def fields(planes, pivot):
    return list(planes) + [planes[pivot] * p for p in planes]


def chunk_operands(v_ref, begin):
    cz = v_ref.shape[3]
    planes = [v_ref[c, pl.ds(begin, CHUNK)].reshape(CHUNK * 8, cz) for c in range(3)]
    return [split(value) for value in fields(planes, 2)]


def edges_kernel(
    steps, v_ref, w_ref, ck_ref, xup_ref, xdn_ref, zup_ref, zdn_ref, wup_ref, wdn_ref, back, fore, mat
):
    s = pl.program_id(0)
    cz = v_ref.shape[3]

    @pl.when(s == 0)
    def _():
        back[...] = jnp.zeros_like(back)
        fore[...] = jnp.zeros_like(fore)
        xup_ref[6:9] = v_ref[:, TX - 1]
        base = w_ref[...]
        lane = lax.broadcasted_iota(jnp.int32, base.shape, 1)
        for f in range(6):
            turned = base if f == 0 else pltpu.roll(base, f, 1)
            mat[2 * f * cz : (2 * f + 1) * cz] = turned.astype(BF16)
            mat[(2 * f + 1) * cz : (2 * f + 2) * cz] = jnp.where(lane < 32, turned, 0.0).astype(BF16)

    ck_ref[0] = back[...]

    def sweep(k, state):
        begin = pl.multiple_of(TX - (k + 1) * CHUNK, CHUNK)
        operands = chunk_operands(v_ref, begin)
        joined = jnp.concatenate([part for pair in operands for part in pair], 1)
        turned = mm(joined, mat[...]).T
        message = turned[0:32] + turned[32:64]
        at = pl.ds(pl.multiple_of(begin * 8, CHUNK * 8), CHUNK * 8)
        zup_ref[:, at] = message[0:8]
        zdn_ref[:, at] = message[16:24]
        spot = pl.ds(TX // CHUNK - 1 - k, 1)
        wup_ref[0, spot] = message[8:9]
        wdn_ref[0, spot] = message[24:25]
        states = list(state)
        for j in range(CHUNK):
            i = begin + (CHUNK - 1 - j)
            now = fields([v_ref[c, i] for c in range(3)], 0)
            states = [ROOT * (f + b) for f, b in zip(now, states)]
        return tuple(states)

    final = lax.fori_loop(0, TX // CHUNK, sweep, tuple(back[c] for c in range(6)))
    for c in range(6):
        back[c] = final[c]
    back[6:9] = v_ref[:, 0]

    @pl.when(s * TX < 128)
    def _():
        def ahead(k, state):
            states = list(state)
            for j in range(STEP):
                i = k * STEP + j
                now = fields([v_ref[c, i] for c in range(3)], 0)
                states = [ROOT * (f + b) for f, b in zip(now, states)]
            return tuple(states)

        zero = jnp.zeros((8, cz), F32)
        ended = lax.fori_loop(0, TX // STEP, ahead, (zero,) * 6)
        scale = jnp.where(s == 0, F32(1.0), F32(ROOT**TX))
        for c in range(6):
            fore[c] = fore[c] + scale * ended[c]

    @pl.when(s == steps - 1)
    def _():
        xup_ref[0:6] = fore[...]
        xdn_ref[...] = back[...]


def find_edges(velocity):
    _, cx, ny, cz = velocity.shape
    steps = cx // TX
    rows = TX * 8
    whole = lambda shape: pl.BlockSpec(shape, lambda s: (0,) * len(shape))
    line = pl.BlockSpec((8, rows), lambda s: (0, steps - 1 - s))
    short = pl.BlockSpec((1, rows // 128, 128), lambda s: (steps - 1 - s, 0, 0))
    return pl.pallas_call(
        functools.partial(edges_kernel, steps),
        grid=(steps,),
        in_specs=[
            pl.BlockSpec((3, TX, 8, cz), lambda s: (0, steps - 1 - s, 0, 0)),
            whole((cz, 128)),
        ],
        out_specs=[
            pl.BlockSpec((1, 9, 8, cz), lambda s: (steps - 1 - s, 0, 0, 0)),
            whole((9, 8, cz)),
            whole((9, 8, cz)),
            line,
            line,
            short,
            short,
        ],
        out_shape=[
            jax.ShapeDtypeStruct((steps, 9, 8, cz), F32),
            jax.ShapeDtypeStruct((9, 8, cz), F32),
            jax.ShapeDtypeStruct((9, 8, cz), F32),
            jax.ShapeDtypeStruct((8, cx * 8), F32),
            jax.ShapeDtypeStruct((8, cx * 8), F32),
            jax.ShapeDtypeStruct((steps, rows // 128, 128), F32),
            jax.ShapeDtypeStruct((steps, rows // 128, 128), F32),
        ],
        scratch_shapes=[
            pltpu.VMEM((9, 8, cz), F32),
            pltpu.VMEM((6, 8, cz), F32),
            pltpu.VMEM((12 * cz, 128), BF16),
        ],
        compiler_params=pltpu.CompilerParams(
            dimension_semantics=("arbitrary",), vmem_limit_bytes=LIMIT
        ),
        name="find_edges",
    )(velocity, jnp.asarray(edge_weights(cz)))


def neighbours_kernel(gx, gz, xup, xdn, zup, zdn, wup, wdn, xl, xr, zl, zr, wl, wr, send_sem, recv_sem):
    mx, mz = lax.axis_index("gx"), lax.axis_index("gz")
    xnext = (lax.rem(mx + 1, gx), mz)
    xlast = (lax.rem(mx + gx - 1, gx), mz)
    znext = (mx, lax.rem(mz + 1, gz))
    zlast = (mx, lax.rem(mz + gz - 1, gz))
    barrier = pltpu.get_barrier_semaphore()
    for peer in (xnext, xlast, znext, zlast):
        pl.semaphore_signal(barrier, inc=1, device_id=peer, device_id_type=MESH)
    pl.semaphore_wait(barrier, 4)
    moves = (
        (zup, zl, znext),
        (zdn, zr, zlast),
        (wup, wl, znext),
        (wdn, wr, zlast),
        (xup, xl, xnext),
        (xdn, xr, xlast),
    )
    copies = []
    for k, (src, dst, peer) in enumerate(moves):
        copy = pltpu.make_async_remote_copy(
            src_ref=src,
            dst_ref=dst,
            send_sem=send_sem.at[k],
            recv_sem=recv_sem.at[k],
            device_id=peer,
            device_id_type=MESH,
        )
        copy.start()
        copies.append(copy)
    for copy in copies:
        copy.wait()


def swap_edges(*arrays):
    gx, gz = lax.axis_size("gx"), lax.axis_size("gz")
    count = len(arrays)
    return pl.pallas_call(
        functools.partial(neighbours_kernel, gx, gz),
        in_specs=[pl.BlockSpec(memory_space=pltpu.VMEM)] * count,
        out_specs=[pl.BlockSpec(memory_space=pltpu.VMEM)] * count,
        out_shape=[jax.ShapeDtypeStruct(a.shape, F32) for a in arrays],
        scratch_shapes=[pltpu.SemaphoreType.DMA((count,)), pltpu.SemaphoreType.DMA((count,))],
        compiler_params=pltpu.CompilerParams(
            collective_id=0, has_side_effects=True, vmem_limit_bytes=8 * 1024 * 1024
        ),
        name="swap_edges",
    )(*arrays)


def main_kernel(
    steps, rp_ref, v_ref, ck_ref, xl_ref, xr_ref, zl_ref, zr_ref, wl_ref, wr_ref, km_ref, cm_ref, sm_ref,
    gx_ref, gz_ref, cv_ref, xs_ref, zs_ref, held, fore, msg,
):
    t = pl.program_id(0)
    cz = v_ref.shape[3]
    rows = TX * 8
    gain = C * ROOT / KAPPA

    @pl.when(t == 0)
    def _():
        for f, edge in enumerate(fields([xl_ref[6 + c] for c in range(3)], 0)):
            fore[f] = C * xl_ref[f]
            fore[6 + f] = KAPPA * edge + C * xl_ref[f]
        xs_ref[...] = jnp.zeros_like(xs_ref)

    parts = []
    for main, short in ((zl_ref, wl_ref), (zr_ref, wr_ref)):
        lines = main[...]
        edge_w = jnp.concatenate([short[0, k : k + 1] for k in range(rows // 128)], 1)
        parts += [lines, edge_w, edge_w * lines[6:7], edge_w * lines[7:8], edge_w * edge_w]
        parts.append(jnp.zeros((4, rows), F32))
    parts = jnp.concatenate(parts, 0)
    high = parts.astype(BF16).astype(F32)
    low = parts - high
    msg[...] = jnp.concatenate([high, low, high, jnp.zeros_like(high)], 0).T.astype(BF16)

    tail = rp_ref[t]
    last = t == steps - 1
    after = [jnp.where(last, xr_ref[6 + c], ck_ref[0, 6 + c]) for c in range(3)]
    start = [C * (ck_ref[0, c] + tail * xr_ref[c]) for c in range(6)]
    shown = [KAPPA * f + b for f, b in zip(fields(after, 0), start)]

    def scaled(i):
        planes = [v_ref[c, i] for c in range(3)]
        scaled_planes = [KAPPA * p for p in planes]
        return scaled_planes + [scaled_planes[0] * p for p in planes]

    def backward(k, state):
        begin = pl.multiple_of(TX - (k + 1) * CHUNK, CHUNK)
        operands = chunk_operands(v_ref, begin)
        joined = jnp.concatenate([jnp.concatenate([hi, hi, lo], 1) for hi, lo in operands], 0)
        slopes = mm(joined, km_ref[...])
        fixes = mm(msg[pl.ds(pl.multiple_of(begin * 8, CHUNK * 8), CHUNK * 8)], cm_ref[...])
        for f in range(6):
            slope = slopes[f * CHUNK * 8 : (f + 1) * CHUNK * 8] + fixes[:, f * cz : (f + 1) * cz]
            target = gz_ref if f < 3 else cv_ref
            target[f % 3, pl.ds(begin, CHUNK)] = slope.reshape(CHUNK, 8, cz)
        states, outs = list(state[:6]), list(state[6:])
        for j in range(CHUNK):
            i = begin + (CHUNK - 1 - j)
            for f in range(6):
                held[f, i] = outs[f]
            now = scaled(i)
            states = [gain * f + ROOT * b for f, b in zip(now, states)]
            outs = [f + b for f, b in zip(now, states)]
        return tuple(states) + tuple(outs)

    lax.fori_loop(0, TX // CHUNK, backward, tuple(start) + tuple(shown))

    def forward(k, state):
        states, outs = list(state[:6]), list(state[6:12])
        sums, moments = state[12], state[13]
        for j in range(STEP):
            i = k * STEP + j
            for f in range(6):
                slope = outs[f] - held[f, i]
                if f < 3:
                    gx_ref[f, i] = slope
                else:
                    cv_ref[f - 3, i] = cv_ref[f - 3, i] + slope
            now = scaled(i)
            states = [gain * f + ROOT * b for f, b in zip(now, states)]
            outs = [f + b for f, b in zip(now, states)]
            w_slope = gz_ref[2, i]
            sums = sums + w_slope
            moments = moments + (t * TX + i).astype(F32) * w_slope
        return tuple(states) + tuple(outs) + (sums, moments)

    begin = tuple(fore[c] for c in range(12))
    ended = lax.fori_loop(0, TX // STEP, forward, begin + (xs_ref[0], xs_ref[1]))
    for c in range(12):
        fore[c] = ended[c]
    xs_ref[0] = ended[12]
    xs_ref[1] = ended[13]

    hi, lo = split(gx_ref[0].reshape(rows, cz))
    sums = (mm(hi, sm_ref[...]) + mm(lo, sm_ref[...])).T
    chunks = [sums[q : q + 1, 128 * k : 128 * k + 128] for q in range(2) for k in range(rows // 128)]
    zs_ref[0] = jnp.concatenate(chunks, 0)


def differentiate(velocity, ck, xl, xr, zl, zr, wl, wr):
    _, cx, ny, cz = velocity.shape
    steps = cx // TX
    rows = TX * 8
    kh, kl = derivative_matrices(cz)
    km = np.concatenate([kh, kl, kh], 0)
    cm = np.concatenate(list(correction_matrices(cz)), 1)
    sm = np.zeros((cz, 128), ml_dtypes.bfloat16)
    sm[:, 0] = 1.0
    sm[:, 1] = np.arange(cz)
    powers = signed_power(TX * (steps - 1 - np.arange(steps))).astype(np.float32)
    whole = lambda shape: pl.BlockSpec(shape, lambda t: (0,) * len(shape))
    tile = pl.BlockSpec((3, TX, 8, cz), lambda t: (0, t, 0, 0))
    line = pl.BlockSpec((8, rows), lambda t: (0, t))
    short = pl.BlockSpec((1, rows // 128, 128), lambda t: (t, 0, 0))
    full = jax.ShapeDtypeStruct(velocity.shape, F32)
    return pl.pallas_call(
        functools.partial(main_kernel, steps),
        grid=(steps,),
        in_specs=[
            pl.BlockSpec(memory_space=pltpu.SMEM),
            tile,
            pl.BlockSpec((1, 9, 8, cz), lambda t: (t, 0, 0, 0)),
            whole((9, 8, cz)),
            whole((9, 8, cz)),
            line,
            line,
            short,
            short,
            whole((3 * cz, cz)),
            whole((128, 6 * cz)),
            whole((cz, 128)),
        ],
        out_specs=[
            tile,
            tile,
            tile,
            whole((2, 8, cz)),
            pl.BlockSpec((1, rows // 64, 128), lambda t: (t, 0, 0)),
        ],
        out_shape=[
            full,
            full,
            full,
            jax.ShapeDtypeStruct((2, 8, cz), F32),
            jax.ShapeDtypeStruct((steps, rows // 64, 128), F32),
        ],
        scratch_shapes=[
            pltpu.VMEM((6, TX, 8, cz), F32),
            pltpu.VMEM((12, 8, cz), F32),
            pltpu.VMEM((rows, 128), BF16),
        ],
        compiler_params=pltpu.CompilerParams(
            dimension_semantics=("arbitrary",), vmem_limit_bytes=LIMIT
        ),
        name="differentiate",
    )(
        jnp.asarray(powers), velocity, ck, xl, xr, zl, zr, wl, wr,
        jnp.asarray(km), jnp.asarray(cm), jnp.asarray(sm),
    )


def gather_kernel(gx, gz, xs, zs, xg, zg, own_sem, send_x, recv_x, send_z, recv_z):
    mx, mz = lax.axis_index("gx"), lax.axis_index("gz")
    xpeers = [(lax.rem(mx + k, gx), mz) for k in range(1, gx)]
    zpeers = [(mx, lax.rem(mz + k, gz)) for k in range(1, gz)]
    barrier = pltpu.get_barrier_semaphore()
    for peer in xpeers + zpeers:
        pl.semaphore_signal(barrier, inc=1, device_id=peer, device_id_type=MESH)
    own = [
        pltpu.make_async_copy(xs, xg.at[mx], own_sem.at[0]),
        pltpu.make_async_copy(zs, zg.at[mz], own_sem.at[1]),
    ]
    for copy in own:
        copy.start()
    pl.semaphore_wait(barrier, gx + gz - 2)
    copies = []
    for src, dst, mine, peers, sends, recvs in (
        (zs, zg, mz, zpeers, send_z, recv_z),
        (xs, xg, mx, xpeers, send_x, recv_x),
    ):
        for k, peer in enumerate(peers):
            copy = pltpu.make_async_remote_copy(
                src_ref=src,
                dst_ref=dst.at[mine],
                send_sem=sends.at[k],
                recv_sem=recvs.at[k],
                device_id=peer,
                device_id_type=MESH,
            )
            copy.start()
            copies.append(copy)
    for copy in own + copies:
        copy.wait()


def gather_sums(xs, zs):
    gx, gz = lax.axis_size("gx"), lax.axis_size("gz")
    dma = pltpu.SemaphoreType.DMA
    return pl.pallas_call(
        functools.partial(gather_kernel, gx, gz),
        in_specs=[pl.BlockSpec(memory_space=pltpu.VMEM)] * 2,
        out_specs=[pl.BlockSpec(memory_space=pltpu.VMEM)] * 2,
        out_shape=[
            jax.ShapeDtypeStruct((gx,) + xs.shape, F32),
            jax.ShapeDtypeStruct((gz,) + zs.shape, F32),
        ],
        scratch_shapes=[
            dma((2,)), dma((gx - 1,)), dma((gx - 1,)), dma((gz - 1,)), dma((gz - 1,))
        ],
        compiler_params=pltpu.CompilerParams(
            collective_id=1, has_side_effects=True, vmem_limit_bytes=8 * 1024 * 1024
        ),
        name="gather_sums",
    )(xs, zs)


def rebuild_kernel(
    nx, nz, wx_ref, wz_ref, xg_ref, zg_ref, tm_ref, pm_ref, gzw_ref, gxu_ref, out_ref, run, mean
):
    t = pl.program_id(0)
    cz = gzw_ref.shape[3]
    rows = TX * 8
    scale_x, scale_z = -1.0 / math.sqrt(nx), -1.0 / math.sqrt(nz)

    @pl.when(t == 0)
    def _():
        base = jnp.zeros((8, cz), F32)
        average = jnp.zeros((8, cz), F32)
        for d in range(xg_ref.shape[0]):
            base = base + wx_ref[d] * xg_ref[d, 0] + xg_ref[d, 1] * (1.0 / nx)
            average = average + xg_ref[d, 0] * (1.0 / nx)
        run[...] = base
        mean[...] = average

    average = mean[...]

    def forward(k, total):
        for j in range(STEP):
            i = k * STEP + j
            value = gzw_ref[0, i]
            out_ref[0, i] = scale_x * (total + 0.5 * value)
            total = total + (value - average)
        return total

    run[...] = lax.fori_loop(0, TX // STEP, forward, run[...])

    chunks = rows // 128
    base = jnp.zeros((chunks, 128), F32)
    slope = jnp.zeros((chunks, 128), F32)
    for d in range(zg_ref.shape[0]):
        block = zg_ref[d, 0]
        base = base + wz_ref[d] * block[0:chunks] + block[chunks:] * (1.0 / nz)
        slope = slope + block[0:chunks] * (1.0 / nz)
    base = jnp.concatenate([base[k : k + 1] for k in range(chunks)], 1)
    slope = jnp.concatenate([slope[k : k + 1] for k in range(chunks)], 1)
    base_high = base.astype(BF16).astype(F32)
    slope_high = slope.astype(BF16).astype(F32)
    stacked = jnp.concatenate(
        [base_high, base - base_high, slope_high, slope - slope_high, jnp.zeros((124, rows), F32)], 0
    )
    message = stacked.T.astype(BF16)
    hi, lo = split(gxu_ref[0].reshape(rows, cz))
    result = mm(hi, tm_ref[...]) + mm(lo, tm_ref[...]) + mm(message, pm_ref[...])
    out_ref[1] = (scale_z * result).reshape(TX, 8, cz)


def start_weights(axis, cells):
    peers, mine = lax.axis_size(axis), lax.axis_index(axis)
    total = peers * cells
    at = jnp.arange(peers)
    starts = (at * cells - mine * cells).astype(F32)
    return (at < mine).astype(F32) + (starts - 0.5 * (total - 1) - 0.5) * (1.0 / total)


def rebuild(grad_x, grad_z, xg, zg):
    _, cx, ny, cz = grad_x.shape
    gx, gz = xg.shape[0], zg.shape[0]
    steps = cx // TX
    rows = TX * 8
    at = np.arange(cz)
    tm = (at[:, None] < at[None, :]) + 0.5 * (at[:, None] == at[None, :])
    pm = np.zeros((128, cz))
    pm[0:2] = 1.0
    pm[2:4] = -at
    whole = lambda shape: pl.BlockSpec(shape, lambda t: (0,) * len(shape))
    return pl.pallas_call(
        functools.partial(rebuild_kernel, cx * gx, cz * gz),
        grid=(steps,),
        in_specs=[
            pl.BlockSpec(memory_space=pltpu.SMEM),
            pl.BlockSpec(memory_space=pltpu.SMEM),
            whole((gx, 2, 8, cz)),
            pl.BlockSpec((gz, 1, rows // 64, 128), lambda t: (0, t, 0, 0)),
            whole((cz, cz)),
            whole((128, cz)),
            pl.BlockSpec((1, TX, 8, cz), lambda t: (2, t, 0, 0)),
            pl.BlockSpec((1, TX, 8, cz), lambda t: (0, t, 0, 0)),
        ],
        out_specs=pl.BlockSpec((2, TX, 8, cz), lambda t: (0, t, 0, 0)),
        out_shape=jax.ShapeDtypeStruct((2, cx, 8, cz), F32),
        scratch_shapes=[pltpu.VMEM((8, cz), F32), pltpu.VMEM((8, cz), F32)],
        compiler_params=pltpu.CompilerParams(
            dimension_semantics=("arbitrary",), vmem_limit_bytes=LIMIT
        ),
        name="rebuild",
    )(
        start_weights("gx", cx), start_weights("gz", cz), xg, zg,
        jnp.asarray(tm.astype(ml_dtypes.bfloat16)), jnp.asarray(pm.astype(ml_dtypes.bfloat16)),
        grad_z, grad_x,
    )


def body(velocity):
    ck, *edges = find_edges(velocity)
    edges = swap_edges(*edges)
    grad_x, grad_z, convect, xs, zs = differentiate(velocity, ck, *edges)
    xg, zg = gather_sums(xs, zs)
    rebuilt = rebuild(grad_x, grad_z, xg, zg)
    return grad_x, grad_z, convect, rebuilt


def solution(mesh):
    placed = P(None, "gx", None, "gz")
    return jax.shard_map(
        body, mesh=mesh, in_specs=(placed,), out_specs=(placed,) * 4, check_vma=False
    )
```

```python
import functools
import math

import jax
import jax.numpy as jnp
import ml_dtypes
import numpy as np
from jax import lax
from jax.experimental import pallas as pl
from jax.experimental.pallas import tpu as pltpu
from jax.sharding import PartitionSpec as P

ROOT = (math.sqrt(5.0) - 3.0) / 2.0
C = 25.0 / 12.0
KAPPA = -1.0 / 12.0
TX = 64
CHUNK = 32
EDGE_CHUNK = 64
STEP = 8
F32 = jnp.float32
BF16 = jnp.bfloat16
LIMIT = 52 * 1024 * 1024
MESH = pl.DeviceIdType.MESH


def halves(array):
    high = array.astype(ml_dtypes.bfloat16)
    low = (array - high.astype(np.float64)).astype(ml_dtypes.bfloat16)
    return high, low


def split(value):
    high = value.astype(BF16)
    low = (value - high.astype(F32)).astype(BF16)
    return high, low


def mm(left, right):
    return jnp.dot(left, right, preferred_element_type=F32)


def kernel_values(offset):
    size = np.abs(offset)
    power = np.power(np.abs(ROOT), size) * np.where(size % 2 == 0, 1.0, -1.0)
    value = np.sign(offset) * C * power
    return value + np.where(size == 1, np.sign(offset) * KAPPA, 0.0)


def signed_power(exponent):
    return np.power(np.abs(ROOT), exponent) * np.where(exponent % 2 == 0, 1.0, -1.0)


def derivative_matrices(cz):
    at = np.arange(cz)
    return halves(kernel_values(at[None, :] - at[:, None]))


def edge_weights(cz):
    at = np.arange(cz)
    base = np.zeros((cz, 32))
    base[:, 0] = signed_power(cz - at)
    base[cz - 1, 6] = 1.0
    base[:, 16] = signed_power(at + 1)
    base[0, 22] = 1.0
    high, low = halves(base)
    out = np.zeros((cz, 128), np.float32)
    out[:, 0:32] = high.astype(np.float32)
    out[:, 32:64] = low.astype(np.float32)
    return out


def correction_matrices(cz):
    at = np.arange(cz)
    out = np.zeros((6, 128, cz))
    for f in range(6):
        base = np.zeros((32, cz))
        base[f] = C * signed_power(at)
        base[6 + f, 0] = KAPPA
        base[16 + f] = -C * signed_power(cz - 1 - at)
        base[22 + f, cz - 1] = -KAPPA
        high, low = halves(base)
        out[f, 0:32] = high.astype(np.float64)
        out[f, 32:64] = high.astype(np.float64)
        out[f, 64:96] = low.astype(np.float64)
    return out.astype(ml_dtypes.bfloat16)


def fields(planes, pivot):
    return list(planes) + [planes[pivot] * p for p in planes]


def chunk_operands(v_ref, begin, count):
    cz = v_ref.shape[3]
    planes = [v_ref[c, pl.ds(begin, count)].reshape(count * 8, cz) for c in range(3)]
    return [split(value) for value in fields(planes, 2)]


def edges_kernel(
    steps, v_ref, w_ref, ck_ref, xup_ref, xdn_ref, zup_ref, zdn_ref, wup_ref, wdn_ref, back, fore, mat
):
    s = pl.program_id(0)
    cz = v_ref.shape[3]

    @pl.when(s == 0)
    def _():
        back[...] = jnp.zeros_like(back)
        fore[...] = jnp.zeros_like(fore)
        xup_ref[6:9] = v_ref[:, TX - 1]
        base = w_ref[...]
        lane = lax.broadcasted_iota(jnp.int32, base.shape, 1)
        for f in range(6):
            turned = base if f == 0 else pltpu.roll(base, f, 1)
            mat[2 * f * cz : (2 * f + 1) * cz] = turned.astype(BF16)
            mat[(2 * f + 1) * cz : (2 * f + 2) * cz] = jnp.where(lane < 32, turned, 0.0).astype(BF16)

    ck_ref[0] = back[...]

    def sweep(k, state):
        begin = pl.multiple_of(TX - (k + 1) * EDGE_CHUNK, EDGE_CHUNK)
        operands = chunk_operands(v_ref, begin, EDGE_CHUNK)
        joined = jnp.concatenate([part for pair in operands for part in pair], 1)
        turned = mm(joined, mat[...]).T
        message = turned[0:32] + turned[32:64]
        at = pl.ds(pl.multiple_of(begin * 8, EDGE_CHUNK * 8), EDGE_CHUNK * 8)
        zup_ref[:, at] = message[0:8]
        zdn_ref[:, at] = message[16:24]
        for q in range(EDGE_CHUNK // 16):
            spot = pl.ds(begin // 16 + q, 1)
            wup_ref[0, spot] = message[8:9, 128 * q : 128 * q + 128]
            wdn_ref[0, spot] = message[24:25, 128 * q : 128 * q + 128]
        states = list(state)
        for j in range(EDGE_CHUNK):
            i = begin + (EDGE_CHUNK - 1 - j)
            now = fields([v_ref[c, i] for c in range(3)], 0)
            states = [ROOT * (f + b) for f, b in zip(now, states)]
        return tuple(states)

    final = lax.fori_loop(0, TX // EDGE_CHUNK, sweep, tuple(back[c] for c in range(6)))
    for c in range(6):
        back[c] = final[c]
    back[6:9] = v_ref[:, 0]

    @pl.when(s * TX < 128)
    def _():
        def ahead(k, state):
            states = list(state)
            for j in range(STEP):
                i = k * STEP + j
                now = fields([v_ref[c, i] for c in range(3)], 0)
                states = [ROOT * (f + b) for f, b in zip(now, states)]
            return tuple(states)

        zero = jnp.zeros((8, cz), F32)
        ended = lax.fori_loop(0, TX // STEP, ahead, (zero,) * 6)
        scale = jnp.where(s == 0, F32(1.0), F32(ROOT**TX))
        for c in range(6):
            fore[c] = fore[c] + scale * ended[c]

    @pl.when(s == steps - 1)
    def _():
        xup_ref[0:6] = fore[...]
        xdn_ref[...] = back[...]


def find_edges(velocity):
    _, cx, ny, cz = velocity.shape
    steps = cx // TX
    rows = TX * 8
    whole = lambda shape: pl.BlockSpec(shape, lambda s: (0,) * len(shape))
    line = pl.BlockSpec((8, rows), lambda s: (0, steps - 1 - s))
    short = pl.BlockSpec((1, rows // 128, 128), lambda s: (steps - 1 - s, 0, 0))
    return pl.pallas_call(
        functools.partial(edges_kernel, steps),
        grid=(steps,),
        in_specs=[
            pl.BlockSpec((3, TX, 8, cz), lambda s: (0, steps - 1 - s, 0, 0)),
            whole((cz, 128)),
        ],
        out_specs=[
            pl.BlockSpec((1, 9, 8, cz), lambda s: (steps - 1 - s, 0, 0, 0)),
            whole((9, 8, cz)),
            whole((9, 8, cz)),
            line,
            line,
            short,
            short,
        ],
        out_shape=[
            jax.ShapeDtypeStruct((steps, 9, 8, cz), F32),
            jax.ShapeDtypeStruct((9, 8, cz), F32),
            jax.ShapeDtypeStruct((9, 8, cz), F32),
            jax.ShapeDtypeStruct((8, cx * 8), F32),
            jax.ShapeDtypeStruct((8, cx * 8), F32),
            jax.ShapeDtypeStruct((steps, rows // 128, 128), F32),
            jax.ShapeDtypeStruct((steps, rows // 128, 128), F32),
        ],
        scratch_shapes=[
            pltpu.VMEM((9, 8, cz), F32),
            pltpu.VMEM((6, 8, cz), F32),
            pltpu.VMEM((12 * cz, 128), BF16),
        ],
        compiler_params=pltpu.CompilerParams(
            dimension_semantics=("arbitrary",), vmem_limit_bytes=LIMIT
        ),
        name="find_edges",
    )(velocity, jnp.asarray(edge_weights(cz)))


def neighbours_kernel(gx, gz, xup, xdn, zup, zdn, wup, wdn, xl, xr, zl, zr, wl, wr, send_sem, recv_sem):
    mx, mz = lax.axis_index("gx"), lax.axis_index("gz")
    xnext = (lax.rem(mx + 1, gx), mz)
    xlast = (lax.rem(mx + gx - 1, gx), mz)
    znext = (mx, lax.rem(mz + 1, gz))
    zlast = (mx, lax.rem(mz + gz - 1, gz))
    barrier = pltpu.get_barrier_semaphore()
    for peer in (xnext, xlast, znext, zlast):
        pl.semaphore_signal(barrier, inc=1, device_id=peer, device_id_type=MESH)
    pl.semaphore_wait(barrier, 4)
    moves = (
        (zup, zl, znext),
        (zdn, zr, zlast),
        (wup, wl, znext),
        (wdn, wr, zlast),
        (xup, xl, xnext),
        (xdn, xr, xlast),
    )
    copies = []
    for k, (src, dst, peer) in enumerate(moves):
        copy = pltpu.make_async_remote_copy(
            src_ref=src,
            dst_ref=dst,
            send_sem=send_sem.at[k],
            recv_sem=recv_sem.at[k],
            device_id=peer,
            device_id_type=MESH,
        )
        copy.start()
        copies.append(copy)
    for copy in copies:
        copy.wait()


def swap_edges(*arrays):
    gx, gz = lax.axis_size("gx"), lax.axis_size("gz")
    count = len(arrays)
    return pl.pallas_call(
        functools.partial(neighbours_kernel, gx, gz),
        in_specs=[pl.BlockSpec(memory_space=pltpu.VMEM)] * count,
        out_specs=[pl.BlockSpec(memory_space=pltpu.VMEM)] * count,
        out_shape=[jax.ShapeDtypeStruct(a.shape, F32) for a in arrays],
        scratch_shapes=[pltpu.SemaphoreType.DMA((count,)), pltpu.SemaphoreType.DMA((count,))],
        compiler_params=pltpu.CompilerParams(
            collective_id=0, has_side_effects=True, vmem_limit_bytes=8 * 1024 * 1024
        ),
        name="swap_edges",
    )(*arrays)


def main_kernel(
    steps, rp_ref, v_ref, ck_ref, xl_ref, xr_ref, zl_ref, zr_ref, wl_ref, wr_ref, km_ref, cm_ref, sm_ref,
    gx_ref, gz_ref, cv_ref, xs_ref, zs_ref, held, fore, msg,
):
    t = pl.program_id(0)
    cz = v_ref.shape[3]
    rows = TX * 8
    gain = C * ROOT / KAPPA

    @pl.when(t == 0)
    def _():
        for f, edge in enumerate(fields([xl_ref[6 + c] for c in range(3)], 0)):
            fore[f] = C * xl_ref[f]
            fore[6 + f] = KAPPA * edge + C * xl_ref[f]
        xs_ref[...] = jnp.zeros_like(xs_ref)

    parts = []
    for main, short in ((zl_ref, wl_ref), (zr_ref, wr_ref)):
        lines = main[...]
        edge_w = jnp.concatenate([short[0, k : k + 1] for k in range(rows // 128)], 1)
        parts += [lines, edge_w, edge_w * lines[6:7], edge_w * lines[7:8], edge_w * edge_w]
        parts.append(jnp.zeros((4, rows), F32))
    parts = jnp.concatenate(parts, 0)
    high = parts.astype(BF16).astype(F32)
    low = parts - high
    msg[...] = jnp.concatenate([high, low, high, jnp.zeros_like(high)], 0).T.astype(BF16)

    tail = rp_ref[t]
    last = t == steps - 1
    after = [jnp.where(last, xr_ref[6 + c], ck_ref[0, 6 + c]) for c in range(3)]
    start = [C * (ck_ref[0, c] + tail * xr_ref[c]) for c in range(6)]
    shown = [KAPPA * f + b for f, b in zip(fields(after, 0), start)]

    def scaled(i):
        planes = [v_ref[c, i] for c in range(3)]
        scaled_planes = [KAPPA * p for p in planes]
        return scaled_planes + [scaled_planes[0] * p for p in planes]

    def backward(k, state):
        begin = pl.multiple_of(TX - (k + 1) * CHUNK, CHUNK)
        operands = chunk_operands(v_ref, begin, CHUNK)
        joined = jnp.concatenate([jnp.concatenate([hi, hi, lo], 1) for hi, lo in operands], 0)
        slopes = mm(joined, km_ref[...])
        fixes = mm(msg[pl.ds(pl.multiple_of(begin * 8, CHUNK * 8), CHUNK * 8)], cm_ref[...])
        for f in range(6):
            slope = slopes[f * CHUNK * 8 : (f + 1) * CHUNK * 8] + fixes[:, f * cz : (f + 1) * cz]
            target = gz_ref if f < 3 else cv_ref
            target[f % 3, pl.ds(begin, CHUNK)] = slope.reshape(CHUNK, 8, cz)
        states, outs = list(state[:6]), list(state[6:])
        for j in range(CHUNK):
            i = begin + (CHUNK - 1 - j)
            for f in range(6):
                held[f, i] = outs[f]
            now = scaled(i)
            states = [gain * f + ROOT * b for f, b in zip(now, states)]
            outs = [f + b for f, b in zip(now, states)]
        return tuple(states) + tuple(outs)

    lax.fori_loop(0, TX // CHUNK, backward, tuple(start) + tuple(shown))

    def forward(k, state):
        states, outs = list(state[:6]), list(state[6:12])
        sums, moments = state[12], state[13]
        for j in range(STEP):
            i = k * STEP + j
            for f in range(6):
                slope = outs[f] - held[f, i]
                if f < 3:
                    gx_ref[f, i] = slope
                else:
                    cv_ref[f - 3, i] = cv_ref[f - 3, i] + slope
            now = scaled(i)
            states = [gain * f + ROOT * b for f, b in zip(now, states)]
            outs = [f + b for f, b in zip(now, states)]
            w_slope = gz_ref[2, i]
            sums = sums + w_slope
            moments = moments + (t * TX + i).astype(F32) * w_slope
        return tuple(states) + tuple(outs) + (sums, moments)

    begin = tuple(fore[c] for c in range(12))
    ended = lax.fori_loop(0, TX // STEP, forward, begin + (xs_ref[0], xs_ref[1]))
    for c in range(12):
        fore[c] = ended[c]
    xs_ref[0] = ended[12]
    xs_ref[1] = ended[13]

    hi, lo = split(gx_ref[0].reshape(rows, cz))
    sums = (mm(hi, sm_ref[...]) + mm(lo, sm_ref[...])).T
    chunks = [sums[q : q + 1, 128 * k : 128 * k + 128] for q in range(2) for k in range(rows // 128)]
    zs_ref[0] = jnp.concatenate(chunks, 0)


def differentiate(velocity, ck, xl, xr, zl, zr, wl, wr):
    _, cx, ny, cz = velocity.shape
    steps = cx // TX
    rows = TX * 8
    kh, kl = derivative_matrices(cz)
    km = np.concatenate([kh, kl, kh], 0)
    cm = np.concatenate(list(correction_matrices(cz)), 1)
    sm = np.zeros((cz, 128), ml_dtypes.bfloat16)
    sm[:, 0] = 1.0
    sm[:, 1] = np.arange(cz)
    powers = signed_power(TX * (steps - 1 - np.arange(steps))).astype(np.float32)
    whole = lambda shape: pl.BlockSpec(shape, lambda t: (0,) * len(shape))
    tile = pl.BlockSpec((3, TX, 8, cz), lambda t: (0, t, 0, 0))
    line = pl.BlockSpec((8, rows), lambda t: (0, t))
    short = pl.BlockSpec((1, rows // 128, 128), lambda t: (t, 0, 0))
    full = jax.ShapeDtypeStruct(velocity.shape, F32)
    return pl.pallas_call(
        functools.partial(main_kernel, steps),
        grid=(steps,),
        in_specs=[
            pl.BlockSpec(memory_space=pltpu.SMEM),
            tile,
            pl.BlockSpec((1, 9, 8, cz), lambda t: (t, 0, 0, 0)),
            whole((9, 8, cz)),
            whole((9, 8, cz)),
            line,
            line,
            short,
            short,
            whole((3 * cz, cz)),
            whole((128, 6 * cz)),
            whole((cz, 128)),
        ],
        out_specs=[
            tile,
            tile,
            tile,
            whole((2, 8, cz)),
            pl.BlockSpec((1, rows // 64, 128), lambda t: (t, 0, 0)),
        ],
        out_shape=[
            full,
            full,
            full,
            jax.ShapeDtypeStruct((2, 8, cz), F32),
            jax.ShapeDtypeStruct((steps, rows // 64, 128), F32),
        ],
        scratch_shapes=[
            pltpu.VMEM((6, TX, 8, cz), F32),
            pltpu.VMEM((12, 8, cz), F32),
            pltpu.VMEM((rows, 128), BF16),
        ],
        compiler_params=pltpu.CompilerParams(
            dimension_semantics=("arbitrary",), vmem_limit_bytes=LIMIT
        ),
        name="differentiate",
    )(
        jnp.asarray(powers), velocity, ck, xl, xr, zl, zr, wl, wr,
        jnp.asarray(km), jnp.asarray(cm), jnp.asarray(sm),
    )


def gather_kernel(gx, gz, xs, zs, xg, zg, own_sem, send_x, recv_x, send_z, recv_z):
    mx, mz = lax.axis_index("gx"), lax.axis_index("gz")
    xpeers = [(lax.rem(mx + k, gx), mz) for k in range(1, gx)]
    zpeers = [(mx, lax.rem(mz + k, gz)) for k in range(1, gz)]
    barrier = pltpu.get_barrier_semaphore()
    for peer in xpeers + zpeers:
        pl.semaphore_signal(barrier, inc=1, device_id=peer, device_id_type=MESH)
    own = [
        pltpu.make_async_copy(xs, xg.at[mx], own_sem.at[0]),
        pltpu.make_async_copy(zs, zg.at[mz], own_sem.at[1]),
    ]
    for copy in own:
        copy.start()
    pl.semaphore_wait(barrier, gx + gz - 2)
    copies = []
    for src, dst, mine, peers, sends, recvs in (
        (zs, zg, mz, zpeers, send_z, recv_z),
        (xs, xg, mx, xpeers, send_x, recv_x),
    ):
        for k, peer in enumerate(peers):
            copy = pltpu.make_async_remote_copy(
                src_ref=src,
                dst_ref=dst.at[mine],
                send_sem=sends.at[k],
                recv_sem=recvs.at[k],
                device_id=peer,
                device_id_type=MESH,
            )
            copy.start()
            copies.append(copy)
    for copy in own + copies:
        copy.wait()


def gather_sums(xs, zs):
    gx, gz = lax.axis_size("gx"), lax.axis_size("gz")
    dma = pltpu.SemaphoreType.DMA
    return pl.pallas_call(
        functools.partial(gather_kernel, gx, gz),
        in_specs=[pl.BlockSpec(memory_space=pltpu.VMEM)] * 2,
        out_specs=[pl.BlockSpec(memory_space=pltpu.VMEM)] * 2,
        out_shape=[
            jax.ShapeDtypeStruct((gx,) + xs.shape, F32),
            jax.ShapeDtypeStruct((gz,) + zs.shape, F32),
        ],
        scratch_shapes=[
            dma((2,)), dma((gx - 1,)), dma((gx - 1,)), dma((gz - 1,)), dma((gz - 1,))
        ],
        compiler_params=pltpu.CompilerParams(
            collective_id=1, has_side_effects=True, vmem_limit_bytes=8 * 1024 * 1024
        ),
        name="gather_sums",
    )(xs, zs)


def rebuild_kernel(
    nx, nz, wx_ref, wz_ref, xg_ref, zg_ref, tm_ref, pm_ref, gzw_ref, gxu_ref, out_ref, run, mean
):
    t = pl.program_id(0)
    cz = gzw_ref.shape[3]
    rows = TX * 8
    scale_x, scale_z = -1.0 / math.sqrt(nx), -1.0 / math.sqrt(nz)

    @pl.when(t == 0)
    def _():
        base = jnp.zeros((8, cz), F32)
        average = jnp.zeros((8, cz), F32)
        for d in range(xg_ref.shape[0]):
            base = base + wx_ref[d] * xg_ref[d, 0] + xg_ref[d, 1] * (1.0 / nx)
            average = average + xg_ref[d, 0] * (1.0 / nx)
        run[...] = base
        mean[...] = average

    average = mean[...]

    def forward(k, total):
        for j in range(STEP):
            i = k * STEP + j
            value = gzw_ref[0, i]
            out_ref[0, i] = scale_x * (total + 0.5 * value)
            total = total + (value - average)
        return total

    run[...] = lax.fori_loop(0, TX // STEP, forward, run[...])

    chunks = rows // 128
    base = jnp.zeros((chunks, 128), F32)
    slope = jnp.zeros((chunks, 128), F32)
    for d in range(zg_ref.shape[0]):
        block = zg_ref[d, 0]
        base = base + wz_ref[d] * block[0:chunks] + block[chunks:] * (1.0 / nz)
        slope = slope + block[0:chunks] * (1.0 / nz)
    base = jnp.concatenate([base[k : k + 1] for k in range(chunks)], 1)
    slope = jnp.concatenate([slope[k : k + 1] for k in range(chunks)], 1)
    base_high = base.astype(BF16).astype(F32)
    slope_high = slope.astype(BF16).astype(F32)
    stacked = jnp.concatenate(
        [base_high, base - base_high, slope_high, slope - slope_high, jnp.zeros((124, rows), F32)], 0
    )
    message = stacked.T.astype(BF16)
    hi, lo = split(gxu_ref[0].reshape(rows, cz))
    result = mm(hi, tm_ref[...]) + mm(lo, tm_ref[...]) + mm(message, pm_ref[...])
    out_ref[1] = (scale_z * result).reshape(TX, 8, cz)


def start_weights(axis, cells):
    peers, mine = lax.axis_size(axis), lax.axis_index(axis)
    total = peers * cells
    at = jnp.arange(peers)
    starts = (at * cells - mine * cells).astype(F32)
    return (at < mine).astype(F32) + (starts - 0.5 * (total - 1) - 0.5) * (1.0 / total)


def rebuild(grad_x, grad_z, xg, zg):
    _, cx, ny, cz = grad_x.shape
    gx, gz = xg.shape[0], zg.shape[0]
    steps = cx // TX
    rows = TX * 8
    at = np.arange(cz)
    tm = (at[:, None] < at[None, :]) + 0.5 * (at[:, None] == at[None, :])
    pm = np.zeros((128, cz))
    pm[0:2] = 1.0
    pm[2:4] = -at
    whole = lambda shape: pl.BlockSpec(shape, lambda t: (0,) * len(shape))
    return pl.pallas_call(
        functools.partial(rebuild_kernel, cx * gx, cz * gz),
        grid=(steps,),
        in_specs=[
            pl.BlockSpec(memory_space=pltpu.SMEM),
            pl.BlockSpec(memory_space=pltpu.SMEM),
            whole((gx, 2, 8, cz)),
            pl.BlockSpec((gz, 1, rows // 64, 128), lambda t: (0, t, 0, 0)),
            whole((cz, cz)),
            whole((128, cz)),
            pl.BlockSpec((1, TX, 8, cz), lambda t: (2, t, 0, 0)),
            pl.BlockSpec((1, TX, 8, cz), lambda t: (0, t, 0, 0)),
        ],
        out_specs=pl.BlockSpec((2, TX, 8, cz), lambda t: (0, t, 0, 0)),
        out_shape=jax.ShapeDtypeStruct((2, cx, 8, cz), F32),
        scratch_shapes=[pltpu.VMEM((8, cz), F32), pltpu.VMEM((8, cz), F32)],
        compiler_params=pltpu.CompilerParams(
            dimension_semantics=("arbitrary",), vmem_limit_bytes=LIMIT
        ),
        name="rebuild",
    )(
        start_weights("gx", cx), start_weights("gz", cz), xg, zg,
        jnp.asarray(tm.astype(ml_dtypes.bfloat16)), jnp.asarray(pm.astype(ml_dtypes.bfloat16)),
        grad_z, grad_x,
    )


def body(velocity):
    ck, *edges = find_edges(velocity)
    edges = swap_edges(*edges)
    grad_x, grad_z, convect, xs, zs = differentiate(velocity, ck, *edges)
    xg, zg = gather_sums(xs, zs)
    rebuilt = rebuild(grad_x, grad_z, xg, zg)
    return grad_x, grad_z, convect, rebuilt


def solution(mesh):
    placed = P(None, "gx", None, "gz")
    return jax.shard_map(
        body, mesh=mesh, in_specs=(placed,), out_specs=(placed,) * 4, check_vma=False
    )
```

```python
import functools
import math

import jax
import jax.numpy as jnp
import ml_dtypes
import numpy as np
from jax import lax
from jax.experimental import pallas as pl
from jax.experimental.pallas import tpu as pltpu
from jax.sharding import PartitionSpec as P

ROOT = (math.sqrt(5.0) - 3.0) / 2.0
C = 25.0 / 12.0
KAPPA = -1.0 / 12.0
TX = 64
CHUNK = 64
EDGE_CHUNK = 64
STEP = 64
F32 = jnp.float32
BF16 = jnp.bfloat16
LIMIT = 52 * 1024 * 1024
MESH = pl.DeviceIdType.MESH


def halves(array):
    high = array.astype(ml_dtypes.bfloat16)
    low = (array - high.astype(np.float64)).astype(ml_dtypes.bfloat16)
    return high, low


def split(value):
    high = value.astype(BF16)
    low = (value - high.astype(F32)).astype(BF16)
    return high, low


def mm(left, right):
    return jnp.dot(left, right, preferred_element_type=F32)


def kernel_values(offset):
    size = np.abs(offset)
    power = np.power(np.abs(ROOT), size) * np.where(size % 2 == 0, 1.0, -1.0)
    value = np.sign(offset) * C * power
    return value + np.where(size == 1, np.sign(offset) * KAPPA, 0.0)


def signed_power(exponent):
    return np.power(np.abs(ROOT), exponent) * np.where(exponent % 2 == 0, 1.0, -1.0)


def derivative_matrices(cz):
    at = np.arange(cz)
    return halves(kernel_values(at[None, :] - at[:, None]))


def edge_weights(cz):
    at = np.arange(cz)
    base = np.zeros((cz, 32))
    base[:, 0] = signed_power(cz - at)
    base[cz - 1, 6] = 1.0
    base[:, 16] = signed_power(at + 1)
    base[0, 22] = 1.0
    high, low = halves(base)
    out = np.zeros((cz, 128), np.float32)
    out[:, 0:32] = high.astype(np.float32)
    out[:, 32:64] = low.astype(np.float32)
    return out


def correction_matrices(cz):
    at = np.arange(cz)
    out = np.zeros((6, 128, cz))
    for f in range(6):
        base = np.zeros((32, cz))
        base[f] = C * signed_power(at)
        base[6 + f, 0] = KAPPA
        base[16 + f] = -C * signed_power(cz - 1 - at)
        base[22 + f, cz - 1] = -KAPPA
        high, low = halves(base)
        out[f, 0:32] = high.astype(np.float64)
        out[f, 32:64] = high.astype(np.float64)
        out[f, 64:96] = low.astype(np.float64)
    return out.astype(ml_dtypes.bfloat16)


def fields(planes, pivot):
    return list(planes) + [planes[pivot] * p for p in planes]


def chunk_operands(v_ref, begin, count):
    cz = v_ref.shape[3]
    planes = [v_ref[c, pl.ds(begin, count)].reshape(count * 8, cz) for c in range(3)]
    return [split(value) for value in fields(planes, 2)]


def edges_kernel(
    steps, v_ref, w_ref, ck_ref, xup_ref, xdn_ref, zup_ref, zdn_ref, wup_ref, wdn_ref, back, fore, mat
):
    s = pl.program_id(0)
    cz = v_ref.shape[3]

    @pl.when(s == 0)
    def _():
        back[...] = jnp.zeros_like(back)
        fore[...] = jnp.zeros_like(fore)
        xup_ref[6:9] = v_ref[:, TX - 1]
        base = w_ref[...]
        lane = lax.broadcasted_iota(jnp.int32, base.shape, 1)
        for f in range(6):
            turned = base if f == 0 else pltpu.roll(base, f, 1)
            mat[2 * f * cz : (2 * f + 1) * cz] = turned.astype(BF16)
            mat[(2 * f + 1) * cz : (2 * f + 2) * cz] = jnp.where(lane < 32, turned, 0.0).astype(BF16)

    ck_ref[0] = back[...]

    def sweep(k, state):
        begin = pl.multiple_of(TX - (k + 1) * EDGE_CHUNK, EDGE_CHUNK)
        operands = chunk_operands(v_ref, begin, EDGE_CHUNK)
        joined = jnp.concatenate([part for pair in operands for part in pair], 1)
        turned = mm(joined, mat[...]).T
        message = turned[0:32] + turned[32:64]
        at = pl.ds(pl.multiple_of(begin * 8, EDGE_CHUNK * 8), EDGE_CHUNK * 8)
        zup_ref[:, at] = message[0:8]
        zdn_ref[:, at] = message[16:24]
        for q in range(EDGE_CHUNK // 16):
            spot = pl.ds(begin // 16 + q, 1)
            wup_ref[0, spot] = message[8:9, 128 * q : 128 * q + 128]
            wdn_ref[0, spot] = message[24:25, 128 * q : 128 * q + 128]
        states = list(state)
        for j in range(EDGE_CHUNK):
            i = begin + (EDGE_CHUNK - 1 - j)
            now = fields([v_ref[c, i] for c in range(3)], 0)
            states = [ROOT * (f + b) for f, b in zip(now, states)]
        return tuple(states)

    final = lax.fori_loop(0, TX // EDGE_CHUNK, sweep, tuple(back[c] for c in range(6)))
    for c in range(6):
        back[c] = final[c]
    back[6:9] = v_ref[:, 0]

    @pl.when(s * TX < 128)
    def _():
        def ahead(k, state):
            states = list(state)
            for j in range(STEP):
                i = k * STEP + j
                now = fields([v_ref[c, i] for c in range(3)], 0)
                states = [ROOT * (f + b) for f, b in zip(now, states)]
            return tuple(states)

        zero = jnp.zeros((8, cz), F32)
        ended = lax.fori_loop(0, TX // STEP, ahead, (zero,) * 6)
        scale = jnp.where(s == 0, F32(1.0), F32(ROOT**TX))
        for c in range(6):
            fore[c] = fore[c] + scale * ended[c]

    @pl.when(s == steps - 1)
    def _():
        xup_ref[0:6] = fore[...]
        xdn_ref[...] = back[...]


def find_edges(velocity):
    _, cx, ny, cz = velocity.shape
    steps = cx // TX
    rows = TX * 8
    whole = lambda shape: pl.BlockSpec(shape, lambda s: (0,) * len(shape))
    line = pl.BlockSpec((8, rows), lambda s: (0, steps - 1 - s))
    short = pl.BlockSpec((1, rows // 128, 128), lambda s: (steps - 1 - s, 0, 0))
    return pl.pallas_call(
        functools.partial(edges_kernel, steps),
        grid=(steps,),
        in_specs=[
            pl.BlockSpec((3, TX, 8, cz), lambda s: (0, steps - 1 - s, 0, 0)),
            whole((cz, 128)),
        ],
        out_specs=[
            pl.BlockSpec((1, 9, 8, cz), lambda s: (steps - 1 - s, 0, 0, 0)),
            whole((9, 8, cz)),
            whole((9, 8, cz)),
            line,
            line,
            short,
            short,
        ],
        out_shape=[
            jax.ShapeDtypeStruct((steps, 9, 8, cz), F32),
            jax.ShapeDtypeStruct((9, 8, cz), F32),
            jax.ShapeDtypeStruct((9, 8, cz), F32),
            jax.ShapeDtypeStruct((8, cx * 8), F32),
            jax.ShapeDtypeStruct((8, cx * 8), F32),
            jax.ShapeDtypeStruct((steps, rows // 128, 128), F32),
            jax.ShapeDtypeStruct((steps, rows // 128, 128), F32),
        ],
        scratch_shapes=[
            pltpu.VMEM((9, 8, cz), F32),
            pltpu.VMEM((6, 8, cz), F32),
            pltpu.VMEM((12 * cz, 128), BF16),
        ],
        compiler_params=pltpu.CompilerParams(
            dimension_semantics=("arbitrary",), vmem_limit_bytes=LIMIT
        ),
        name="find_edges",
    )(velocity, jnp.asarray(edge_weights(cz)))


def neighbours_kernel(gx, gz, xup, xdn, zup, zdn, wup, wdn, xl, xr, zl, zr, wl, wr, send_sem, recv_sem):
    mx, mz = lax.axis_index("gx"), lax.axis_index("gz")
    xnext = (lax.rem(mx + 1, gx), mz)
    xlast = (lax.rem(mx + gx - 1, gx), mz)
    znext = (mx, lax.rem(mz + 1, gz))
    zlast = (mx, lax.rem(mz + gz - 1, gz))
    barrier = pltpu.get_barrier_semaphore()
    for peer in (xnext, xlast, znext, zlast):
        pl.semaphore_signal(barrier, inc=1, device_id=peer, device_id_type=MESH)
    pl.semaphore_wait(barrier, 4)
    moves = (
        (zup, zl, znext),
        (zdn, zr, zlast),
        (wup, wl, znext),
        (wdn, wr, zlast),
        (xup, xl, xnext),
        (xdn, xr, xlast),
    )
    copies = []
    for k, (src, dst, peer) in enumerate(moves):
        copy = pltpu.make_async_remote_copy(
            src_ref=src,
            dst_ref=dst,
            send_sem=send_sem.at[k],
            recv_sem=recv_sem.at[k],
            device_id=peer,
            device_id_type=MESH,
        )
        copy.start()
        copies.append(copy)
    for copy in copies:
        copy.wait()


def swap_edges(*arrays):
    gx, gz = lax.axis_size("gx"), lax.axis_size("gz")
    count = len(arrays)
    return pl.pallas_call(
        functools.partial(neighbours_kernel, gx, gz),
        in_specs=[pl.BlockSpec(memory_space=pltpu.VMEM)] * count,
        out_specs=[pl.BlockSpec(memory_space=pltpu.VMEM)] * count,
        out_shape=[jax.ShapeDtypeStruct(a.shape, F32) for a in arrays],
        scratch_shapes=[pltpu.SemaphoreType.DMA((count,)), pltpu.SemaphoreType.DMA((count,))],
        compiler_params=pltpu.CompilerParams(
            collective_id=0, has_side_effects=True, vmem_limit_bytes=8 * 1024 * 1024
        ),
        name="swap_edges",
    )(*arrays)


def main_kernel(
    steps, rp_ref, v_ref, ck_ref, xl_ref, xr_ref, zl_ref, zr_ref, wl_ref, wr_ref, km_ref, cm_ref, sm_ref,
    gx_ref, gz_ref, cv_ref, xs_ref, zs_ref, held, fore, msg,
):
    t = pl.program_id(0)
    cz = v_ref.shape[3]
    rows = TX * 8
    gain = C * ROOT / KAPPA

    @pl.when(t == 0)
    def _():
        for f, edge in enumerate(fields([xl_ref[6 + c] for c in range(3)], 0)):
            fore[f] = C * xl_ref[f]
            fore[6 + f] = KAPPA * edge + C * xl_ref[f]
        xs_ref[...] = jnp.zeros_like(xs_ref)

    parts = []
    for main, short in ((zl_ref, wl_ref), (zr_ref, wr_ref)):
        lines = main[...]
        edge_w = jnp.concatenate([short[0, k : k + 1] for k in range(rows // 128)], 1)
        parts += [lines, edge_w, edge_w * lines[6:7], edge_w * lines[7:8], edge_w * edge_w]
        parts.append(jnp.zeros((4, rows), F32))
    parts = jnp.concatenate(parts, 0)
    high = parts.astype(BF16).astype(F32)
    low = parts - high
    msg[...] = jnp.concatenate([high, low, high, jnp.zeros_like(high)], 0).T.astype(BF16)

    tail = rp_ref[t]
    last = t == steps - 1
    after = [jnp.where(last, xr_ref[6 + c], ck_ref[0, 6 + c]) for c in range(3)]
    start = [C * (ck_ref[0, c] + tail * xr_ref[c]) for c in range(6)]
    shown = [KAPPA * f + b for f, b in zip(fields(after, 0), start)]

    def scaled(i):
        planes = [v_ref[c, i] for c in range(3)]
        scaled_planes = [KAPPA * p for p in planes]
        return scaled_planes + [scaled_planes[0] * p for p in planes]

    def backward(k, state):
        begin = pl.multiple_of(TX - (k + 1) * CHUNK, CHUNK)
        operands = chunk_operands(v_ref, begin, CHUNK)
        joined = jnp.concatenate([jnp.concatenate([hi, hi, lo], 1) for hi, lo in operands], 0)
        slopes = mm(joined, km_ref[...])
        fixes = mm(msg[pl.ds(pl.multiple_of(begin * 8, CHUNK * 8), CHUNK * 8)], cm_ref[...])
        for f in range(6):
            slope = slopes[f * CHUNK * 8 : (f + 1) * CHUNK * 8] + fixes[:, f * cz : (f + 1) * cz]
            target = gz_ref if f < 3 else cv_ref
            target[f % 3, pl.ds(begin, CHUNK)] = slope.reshape(CHUNK, 8, cz)
        states, outs = list(state[:6]), list(state[6:])
        for j in range(CHUNK):
            i = begin + (CHUNK - 1 - j)
            for f in range(6):
                held[f, i] = outs[f]
            now = scaled(i)
            states = [gain * f + ROOT * b for f, b in zip(now, states)]
            outs = [f + b for f, b in zip(now, states)]
        return tuple(states) + tuple(outs)

    lax.fori_loop(0, TX // CHUNK, backward, tuple(start) + tuple(shown))

    def forward(k, state):
        states, outs = list(state[:6]), list(state[6:12])
        sums, moments = state[12], state[13]
        for j in range(STEP):
            i = k * STEP + j
            for f in range(6):
                slope = outs[f] - held[f, i]
                if f < 3:
                    gx_ref[f, i] = slope
                else:
                    cv_ref[f - 3, i] = cv_ref[f - 3, i] + slope
            now = scaled(i)
            states = [gain * f + ROOT * b for f, b in zip(now, states)]
            outs = [f + b for f, b in zip(now, states)]
            w_slope = gz_ref[2, i]
            sums = sums + w_slope
            moments = moments + (t * TX + i).astype(F32) * w_slope
        return tuple(states) + tuple(outs) + (sums, moments)

    begin = tuple(fore[c] for c in range(12))
    ended = lax.fori_loop(0, TX // STEP, forward, begin + (xs_ref[0], xs_ref[1]))
    for c in range(12):
        fore[c] = ended[c]
    xs_ref[0] = ended[12]
    xs_ref[1] = ended[13]

    hi, lo = split(gx_ref[0].reshape(rows, cz))
    sums = (mm(hi, sm_ref[...]) + mm(lo, sm_ref[...])).T
    chunks = [sums[q : q + 1, 128 * k : 128 * k + 128] for q in range(2) for k in range(rows // 128)]
    zs_ref[0] = jnp.concatenate(chunks, 0)


def differentiate(velocity, ck, xl, xr, zl, zr, wl, wr):
    _, cx, ny, cz = velocity.shape
    steps = cx // TX
    rows = TX * 8
    kh, kl = derivative_matrices(cz)
    km = np.concatenate([kh, kl, kh], 0)
    cm = np.concatenate(list(correction_matrices(cz)), 1)
    sm = np.zeros((cz, 128), ml_dtypes.bfloat16)
    sm[:, 0] = 1.0
    sm[:, 1] = np.arange(cz)
    powers = signed_power(TX * (steps - 1 - np.arange(steps))).astype(np.float32)
    whole = lambda shape: pl.BlockSpec(shape, lambda t: (0,) * len(shape))
    tile = pl.BlockSpec((3, TX, 8, cz), lambda t: (0, t, 0, 0))
    line = pl.BlockSpec((8, rows), lambda t: (0, t))
    short = pl.BlockSpec((1, rows // 128, 128), lambda t: (t, 0, 0))
    full = jax.ShapeDtypeStruct(velocity.shape, F32)
    return pl.pallas_call(
        functools.partial(main_kernel, steps),
        grid=(steps,),
        in_specs=[
            pl.BlockSpec(memory_space=pltpu.SMEM),
            tile,
            pl.BlockSpec((1, 9, 8, cz), lambda t: (t, 0, 0, 0)),
            whole((9, 8, cz)),
            whole((9, 8, cz)),
            line,
            line,
            short,
            short,
            whole((3 * cz, cz)),
            whole((128, 6 * cz)),
            whole((cz, 128)),
        ],
        out_specs=[
            tile,
            tile,
            tile,
            whole((2, 8, cz)),
            pl.BlockSpec((1, rows // 64, 128), lambda t: (t, 0, 0)),
        ],
        out_shape=[
            full,
            full,
            full,
            jax.ShapeDtypeStruct((2, 8, cz), F32),
            jax.ShapeDtypeStruct((steps, rows // 64, 128), F32),
        ],
        scratch_shapes=[
            pltpu.VMEM((6, TX, 8, cz), F32),
            pltpu.VMEM((12, 8, cz), F32),
            pltpu.VMEM((rows, 128), BF16),
        ],
        compiler_params=pltpu.CompilerParams(
            dimension_semantics=("arbitrary",), vmem_limit_bytes=LIMIT
        ),
        name="differentiate",
    )(
        jnp.asarray(powers), velocity, ck, xl, xr, zl, zr, wl, wr,
        jnp.asarray(km), jnp.asarray(cm), jnp.asarray(sm),
    )


def gather_kernel(gx, gz, xs, zs, xg, zg, own_sem, send_x, recv_x, send_z, recv_z):
    mx, mz = lax.axis_index("gx"), lax.axis_index("gz")
    xpeers = [(lax.rem(mx + k, gx), mz) for k in range(1, gx)]
    zpeers = [(mx, lax.rem(mz + k, gz)) for k in range(1, gz)]
    barrier = pltpu.get_barrier_semaphore()
    for peer in xpeers + zpeers:
        pl.semaphore_signal(barrier, inc=1, device_id=peer, device_id_type=MESH)
    own = [
        pltpu.make_async_copy(xs, xg.at[mx], own_sem.at[0]),
        pltpu.make_async_copy(zs, zg.at[mz], own_sem.at[1]),
    ]
    for copy in own:
        copy.start()
    pl.semaphore_wait(barrier, gx + gz - 2)
    copies = []
    for src, dst, mine, peers, sends, recvs in (
        (zs, zg, mz, zpeers, send_z, recv_z),
        (xs, xg, mx, xpeers, send_x, recv_x),
    ):
        for k, peer in enumerate(peers):
            copy = pltpu.make_async_remote_copy(
                src_ref=src,
                dst_ref=dst.at[mine],
                send_sem=sends.at[k],
                recv_sem=recvs.at[k],
                device_id=peer,
                device_id_type=MESH,
            )
            copy.start()
            copies.append(copy)
    for copy in own + copies:
        copy.wait()


def gather_sums(xs, zs):
    gx, gz = lax.axis_size("gx"), lax.axis_size("gz")
    dma = pltpu.SemaphoreType.DMA
    return pl.pallas_call(
        functools.partial(gather_kernel, gx, gz),
        in_specs=[pl.BlockSpec(memory_space=pltpu.VMEM)] * 2,
        out_specs=[pl.BlockSpec(memory_space=pltpu.VMEM)] * 2,
        out_shape=[
            jax.ShapeDtypeStruct((gx,) + xs.shape, F32),
            jax.ShapeDtypeStruct((gz,) + zs.shape, F32),
        ],
        scratch_shapes=[
            dma((2,)), dma((gx - 1,)), dma((gx - 1,)), dma((gz - 1,)), dma((gz - 1,))
        ],
        compiler_params=pltpu.CompilerParams(
            collective_id=1, has_side_effects=True, vmem_limit_bytes=8 * 1024 * 1024
        ),
        name="gather_sums",
    )(xs, zs)


def rebuild_kernel(
    nx, nz, wx_ref, wz_ref, xg_ref, zg_ref, tm_ref, pm_ref, gzw_ref, gxu_ref, out_ref, run, mean
):
    t = pl.program_id(0)
    cz = gzw_ref.shape[3]
    rows = TX * 8
    scale_x, scale_z = -1.0 / math.sqrt(nx), -1.0 / math.sqrt(nz)

    @pl.when(t == 0)
    def _():
        base = jnp.zeros((8, cz), F32)
        average = jnp.zeros((8, cz), F32)
        for d in range(xg_ref.shape[0]):
            base = base + wx_ref[d] * xg_ref[d, 0] + xg_ref[d, 1] * (1.0 / nx)
            average = average + xg_ref[d, 0] * (1.0 / nx)
        run[...] = base
        mean[...] = average

    average = mean[...]

    def forward(k, total):
        for j in range(STEP):
            i = k * STEP + j
            value = gzw_ref[0, i]
            out_ref[0, i] = scale_x * (total + 0.5 * value)
            total = total + (value - average)
        return total

    run[...] = lax.fori_loop(0, TX // STEP, forward, run[...])

    chunks = rows // 128
    base = jnp.zeros((chunks, 128), F32)
    slope = jnp.zeros((chunks, 128), F32)
    for d in range(zg_ref.shape[0]):
        block = zg_ref[d, 0]
        base = base + wz_ref[d] * block[0:chunks] + block[chunks:] * (1.0 / nz)
        slope = slope + block[0:chunks] * (1.0 / nz)
    base = jnp.concatenate([base[k : k + 1] for k in range(chunks)], 1)
    slope = jnp.concatenate([slope[k : k + 1] for k in range(chunks)], 1)
    base_high = base.astype(BF16).astype(F32)
    slope_high = slope.astype(BF16).astype(F32)
    stacked = jnp.concatenate(
        [base_high, base - base_high, slope_high, slope - slope_high, jnp.zeros((124, rows), F32)], 0
    )
    message = stacked.T.astype(BF16)
    hi, lo = split(gxu_ref[0].reshape(rows, cz))
    result = mm(hi, tm_ref[...]) + mm(lo, tm_ref[...]) + mm(message, pm_ref[...])
    out_ref[1] = (scale_z * result).reshape(TX, 8, cz)


def start_weights(axis, cells):
    peers, mine = lax.axis_size(axis), lax.axis_index(axis)
    total = peers * cells
    at = jnp.arange(peers)
    starts = (at * cells - mine * cells).astype(F32)
    return (at < mine).astype(F32) + (starts - 0.5 * (total - 1) - 0.5) * (1.0 / total)


def rebuild(grad_x, grad_z, xg, zg):
    _, cx, ny, cz = grad_x.shape
    gx, gz = xg.shape[0], zg.shape[0]
    steps = cx // TX
    rows = TX * 8
    at = np.arange(cz)
    tm = (at[:, None] < at[None, :]) + 0.5 * (at[:, None] == at[None, :])
    pm = np.zeros((128, cz))
    pm[0:2] = 1.0
    pm[2:4] = -at
    whole = lambda shape: pl.BlockSpec(shape, lambda t: (0,) * len(shape))
    return pl.pallas_call(
        functools.partial(rebuild_kernel, cx * gx, cz * gz),
        grid=(steps,),
        in_specs=[
            pl.BlockSpec(memory_space=pltpu.SMEM),
            pl.BlockSpec(memory_space=pltpu.SMEM),
            whole((gx, 2, 8, cz)),
            pl.BlockSpec((gz, 1, rows // 64, 128), lambda t: (0, t, 0, 0)),
            whole((cz, cz)),
            whole((128, cz)),
            pl.BlockSpec((1, TX, 8, cz), lambda t: (2, t, 0, 0)),
            pl.BlockSpec((1, TX, 8, cz), lambda t: (0, t, 0, 0)),
        ],
        out_specs=pl.BlockSpec((2, TX, 8, cz), lambda t: (0, t, 0, 0)),
        out_shape=jax.ShapeDtypeStruct((2, cx, 8, cz), F32),
        scratch_shapes=[pltpu.VMEM((8, cz), F32), pltpu.VMEM((8, cz), F32)],
        compiler_params=pltpu.CompilerParams(
            dimension_semantics=("arbitrary",), vmem_limit_bytes=LIMIT
        ),
        name="rebuild",
    )(
        start_weights("gx", cx), start_weights("gz", cz), xg, zg,
        jnp.asarray(tm.astype(ml_dtypes.bfloat16)), jnp.asarray(pm.astype(ml_dtypes.bfloat16)),
        grad_z, grad_x,
    )


def body(velocity):
    ck, *edges = find_edges(velocity)
    edges = swap_edges(*edges)
    grad_x, grad_z, convect, xs, zs = differentiate(velocity, ck, *edges)
    xg, zg = gather_sums(xs, zs)
    rebuilt = rebuild(grad_x, grad_z, xg, zg)
    return grad_x, grad_z, convect, rebuilt


def solution(mesh):
    placed = P(None, "gx", None, "gz")
    return jax.shard_map(
        body, mesh=mesh, in_specs=(placed,), out_specs=(placed,) * 4, check_vma=False
    )
```
